256 devices in a mesh: tm: 64 (over z, y_hi, x), sta: 4 (over y_lo, core).
Axes of the slice: x: 4, y: 4 (y_hi: 2, y_lo: 2; y = y_hi * 2 + y_lo), z: 8, core: 2. Of those that a mesh axis runs over, the one named last changes fastest.
Arguments:
- data: bfloat16 [288, 131072], P('sta', 'tm'), may hold values from -6 to 6
- bank: bfloat16 [64, 288, 1024], P('tm', 'sta'), may hold values from -6 to 6
- select: int32 [4], replicated, may hold values from 0 to 63
- shifts: int32 [4, 288], P(None, 'sta'), may hold values from 0 to 255
Outputs:
- detection: float32 [4, 131072], P('sta', 'tm')
The draws below stay inside these ranges and needn't reach their ends.
All inputs are finite; a program needn't handle non-finite values. Where the reference program divides by a largest or mean magnitude, that divisor is 1e-20 or more.
Results may differ from the reference program's by a relative error of at most 0.0029.
Values may be sent and summed in bfloat16 or wider, within the bound.
A program may use at most 64 MiB of HBM per device.

```python
import jax
import jax.numpy as jnp
from jax import lax

CH = 288
TL = 1024
K = 4
MAXSHIFT = 256
TIME = 131072
BANK = 64


def set_ends(drawn, stream_key, least, high):
    extent = drawn.shape
    index_at = [jax.random.randint(jax.random.fold_in(stream_key, axis), (), 0, extent[axis]) for axis in range(len(extent))]
    drawn = drawn.at[tuple(index_at)].set(least)
    longest = extent.index(max(extent))
    index_at[longest] = (index_at[longest] + 1) % extent[longest]
    return drawn.at[tuple(index_at)].set(high)


def level_of(own_key, dims, pieces, low, top_value):
    loudness = 1.0
    for axis_at, blocks in pieces:
        draws = jax.random.uniform(jax.random.fold_in(jax.random.fold_in(own_key, 6), axis_at), (blocks,), jnp.float32, low / len(pieces), top_value / len(pieces))
        loudness = loudness * jnp.repeat(jnp.exp(draws), dims[axis_at] // blocks).reshape((-1,) + (1,) * (len(dims) - 1 - axis_at))
    return loudness


def normal_values(key, shape, spread, bound, pieces=(), held_as=jnp.bfloat16):
    array = jax.random.normal(key, shape, jnp.float32) * spread
    if len(pieces) > 0:
        array = level_of(key, shape, pieces, -0.22, 0.18) * array
    return jnp.clip(array, min=-bound, max=bound).astype(held_as)


def setup_inputs(seed: int = 0) -> dict:
    seeds = jax.random.split(jax.random.key(seed), 5)
    return {
        "data": normal_values(seeds[0], (CH, TIME), 1.0, 6.0, ((0, 4), (1, 64))),
        "bank": normal_values(seeds[1], (BANK, CH, TL), 1.0, 6.0, ((0, 64), (1, 4))),
        "select": set_ends(jax.random.randint(seeds[2], (K,), 0, BANK), jax.random.fold_in(seeds[2], 1), 0, BANK - 1).astype(jnp.int32),
        "shifts": set_ends(jax.random.randint(seeds[3], (K, CH), 0, MAXSHIFT), jax.random.fold_in(seeds[3], 1), 0, MAXSHIFT - 1).astype(jnp.int32),
    }


def window_sums(values, out_length):
    width = 32
    span = TL // width
    nblocks = (out_length + TL) // width
    starts = out_length // width
    lead = values.shape[:-1]
    blocks = values[..., :nblocks * width].reshape(lead + (nblocks, width))
    inner_sums = jnp.cumsum(blocks, axis=-1) - blocks
    block_totals = lax.optimization_barrier(jnp.sum(blocks, axis=-1))
    running = jnp.concatenate([jnp.zeros(lead + (1,), jnp.float32), jnp.cumsum(block_totals, axis=-1)], axis=-1)
    whole_span = running[..., span:span + starts] - running[..., :starts]
    result = whole_span[..., None] - inner_sums[..., :starts, :] + inner_sums[..., span:span + starts, :]
    return result.reshape(lead + (out_length,))

def normalize_templates(rows):
    centred = rows - lax.optimization_barrier(jnp.mean(rows, axis=-1, keepdims=True))
    factor = lax.rsqrt(lax.optimization_barrier(jnp.sum(centred * centred, axis=-1, keepdims=True)) + 1e-05)
    return (centred * factor).astype(jnp.bfloat16)

def reference(data, bank, select, shifts):
    chosen = bank[select]
    templates_n = normalize_templates(chosen.astype(jnp.float32))
    extended = jnp.pad(data.astype(jnp.float32), ((0, 0), (0, TL + MAXSHIFT)))
    out_length = TIME + MAXSHIFT
    window_sum = window_sums(extended, out_length)
    window_sq = window_sums(extended * extended, out_length)
    scale_rows = lax.rsqrt(jnp.maximum(window_sq - window_sum * window_sum / TL, TL / 8.0))
    fft_length = 1 << (extended.shape[1] - 1).bit_length()
    spectrum = jnp.fft.rfft(extended, fft_length, axis=1)

    def one_template(paired):
        rows, offsets = paired
        tspec = jnp.fft.rfft(rows.astype(jnp.float32), fft_length, axis=1)
        correl = jnp.fft.irfft(spectrum * jnp.conj(tspec), fft_length, axis=1)[:, :out_length]
        normed = correl * scale_rows
        moved = jax.vmap(lambda series, offset: lax.dynamic_slice_in_dim(series, offset, TIME))(normed, offsets)
        return lax.optimization_barrier(jnp.sum(moved, axis=0))
    stacks = lax.map(one_template, (templates_n, shifts))
    peaks = lax.optimization_barrier(jnp.max(jnp.abs(stacks), axis=1, keepdims=True))
    return stacks / (peaks + 1e-06)
```

```python
import jax
import jax.numpy as jnp
from jax import lax
from jax.experimental import pallas as pl
from jax.experimental.pallas import tpu as pltpu
from jax.sharding import PartitionSpec as P

TL = 1024
B = 128
GROUP = 8
PIECE = 16
OUT_ROWS = GROUP * PIECE
ROWS = OUT_ROWS + 8
ALL_ROWS = ROWS + 8
LAGS = TL // B + 1
K = 4
MESH = pl.DeviceIdType.MESH
f32, bf16 = jnp.float32, jnp.bfloat16


def place():
    me = lax.axis_index("tm")
    z = lax.div(me, GROUP)
    return z, me - z * GROUP, lax.axis_size("tm") // GROUP


def others(mine, count, shift=1):
    return [lax.rem(mine + shift * i + count, count) for i in range(1, count)]


def greet(devices):
    barrier = pltpu.get_barrier_semaphore()
    for device in devices:
        pl.semaphore_signal(barrier, inc=1, device_id=device, device_id_type=MESH)
    pl.semaphore_wait(barrier, len(devices))


def remote(src, dst, send_sem, recv_sem, device):
    return pltpu.make_async_remote_copy(
        src_ref=src, dst_ref=dst, send_sem=send_sem, recv_sem=recv_sem, device_id=device, device_id_type=MESH
    )


def fetch_kernel(select_ref, data_ref, bank_ref, rows_ref, tpl_ref, raw, part, got, sems, own_sems):
    z, p, depth = place()
    per = data_ref.shape[0] // GROUP
    in_group = lambda q: {"tm": z * GROUP + q}
    in_depth = lambda w: {"tm": w * GROUP + p}
    greet([in_group(q) for q in others(p, GROUP)] + [in_depth(w) for w in others(z, depth)])

    own_data = pltpu.make_async_copy(data_ref.at[pl.ds(p * per, per)], rows_ref.at[p], own_sems.at[0])
    own_bank = pltpu.make_async_copy(bank_ref.at[pl.ds(p * per, per)], raw.at[p], own_sems.at[1])
    own_bank.start()
    own_data.start()

    def bank_copy(owner, q):
        return remote(bank_ref.at[pl.ds(q * per, per)], raw.at[owner], sems.at[0, q], sems.at[1, owner], in_group(q))

    def data_copy(owner, q):
        return remote(data_ref.at[pl.ds(q * per, per)], rows_ref.at[owner], sems.at[2, q], sems.at[3, owner], in_group(q))

    def part_copy(owner, w):
        return remote(part.at[w], got.at[owner], sems.at[4, w], sems.at[5, owner], in_depth(w))

    def tpl_copy(owner, w):
        return remote(tpl_ref.at[owner], tpl_ref.at[owner], sems.at[6, w], sems.at[7, owner], in_depth(w))

    for q in others(p, GROUP):
        bank_copy(p, q).start()
    for q in others(p, GROUP):
        data_copy(p, q).start()

    own_bank.wait()
    for q in others(p, GROUP, -1):
        bank_copy(q, p).wait_recv()
    for k in range(K):
        wanted = select_ref[k] - z * GROUP
        picked = jnp.zeros(raw.shape[1:], f32)
        for j in range(GROUP):
            picked += jnp.where(wanted == j, raw[j].astype(f32), 0.0)
        picked = picked.astype(bf16)
        for half in range(2):
            part[2 * k + half] = picked[4 * half : 4 * half + 5]
    for w in others(z, depth):
        part_copy(z, w).start()
    got[z] = part[z]

    own_data.wait()
    for q in others(p, GROUP, -1):
        data_copy(q, p).wait_recv()
    before, after = lax.rem(z + depth - 1, depth), lax.rem(z + 1, depth)
    halo = remote(rows_ref.at[0], rows_ref.at[GROUP], own_sems.at[2], own_sems.at[3], in_depth(before))
    halo.start()

    for w in others(z, depth, -1):
        part_copy(w, z).wait_recv()
    tpl = got[0].astype(f32)
    for j in range(1, GROUP):
        tpl += got[j].astype(f32)
    mean = jnp.sum(jnp.sum(tpl, axis=2, keepdims=True), axis=1, keepdims=True) / TL
    centred = tpl - mean
    power = jnp.sum(jnp.sum(centred * centred, axis=2, keepdims=True), axis=1, keepdims=True)
    normed = (centred * lax.rsqrt(power + 1e-05)).astype(bf16)
    tpl_ref[z] = normed
    for w in others(z, depth):
        tpl_copy(z, w).start()
    for w in others(z, depth, -1):
        tpl_copy(w, z).wait_recv()
    halo.wait()
    for q in others(p, GROUP):
        bank_copy(p, q).wait_send()
        data_copy(p, q).wait_send()
    for w in others(z, depth):
        part_copy(z, w).wait_send()
        tpl_copy(z, w).wait_send()


def fetch(select, data, bank):
    per = data.shape[0] // GROUP
    vmem = pl.BlockSpec(memory_space=pltpu.VMEM)
    return pl.pallas_call(
        fetch_kernel,
        out_shape=[
            jax.ShapeDtypeStruct((GROUP + 1, per, PIECE, B), bf16),
            jax.ShapeDtypeStruct((2 * K, 5, TL // B, B), bf16),
        ],
        in_specs=[pl.BlockSpec(memory_space=pltpu.SMEM), vmem, vmem],
        out_specs=[vmem, vmem],
        scratch_shapes=[
            pltpu.VMEM((GROUP, per, TL // B, B), bf16),
            pltpu.VMEM((2 * K, 5, TL // B, B), bf16),
            pltpu.VMEM((2 * K, 5, TL // B, B), bf16),
            pltpu.SemaphoreType.DMA((8, GROUP)),
            pltpu.SemaphoreType.DMA((4,)),
        ],
        compiler_params=pltpu.CompilerParams(
            collective_id=0, has_side_effects=True, vmem_limit_bytes=16 * 2**20
        ),
    )(select, data, bank)


def correlate_kernel(rows_ref, tpl_ref, shifts_ref, out_ref, x_ref, toeplitz, moved):
    z, p, depth = place()
    per = rows_ref.shape[1]
    row = lax.broadcasted_iota(jnp.int32, (ALL_ROWS, B), 0)
    lane = lax.broadcasted_iota(jnp.int32, (OUT_ROWS, B), 1)
    before = lax.broadcasted_iota(jnp.int32, (B, 2 * B), 0) < lax.broadcasted_iota(jnp.int32, (B, 2 * B), 1)
    sums = jnp.where(before, 1.0, 0.0).astype(bf16)
    flip_at = lax.broadcasted_iota(jnp.int32, (B, B), 0) + lax.broadcasted_iota(jnp.int32, (B, B), 1)
    flip = jnp.where(flip_at == B - 1, 1.0, 0.0).astype(bf16)
    valid = jnp.where(z == depth - 1, OUT_ROWS, ALL_ROWS)
    out_ref[...] = jnp.zeros_like(out_ref)

    def dot(a, b):
        return jnp.dot(a, b, preferred_element_type=f32)

    def windows(v):
        ahead, total = v[:, :B], v[:, B:]
        two = total[0:143] + total[1:144]
        four = two[0:141] + two[2:143]
        eight = four[0:136] + four[4:140]
        return eight - ahead[0:136] + ahead[8:144]

    def channel(c, carry):
        x = jnp.where(row < valid, rows_ref[:, c].astype(f32).reshape(ALL_ROWS, B), 0.0)
        x_ref[...] = x
        square = x * x
        high = square.astype(bf16)
        low = (square - high.astype(f32)).astype(bf16)
        window_sum = windows(dot(x.astype(bf16), sums))
        window_sq = windows(dot(high, sums) + dot(low, sums))
        scale = lax.rsqrt(jnp.maximum(window_sq - window_sum * window_sum / TL, TL / 8.0))
        half = lax.div(c, 5)
        zero = jnp.zeros((1, B), f32)
        for k in range(K):
            tpl = dot(tpl_ref[2 * k + half, c - 4 * half], flip)
            line = jnp.concatenate([zero] + [tpl[7 - m : 8 - m] for m in range(TL // B)] + [zero], axis=1)
            for g in range(0, B, 16):
                wide = jnp.broadcast_to(line, (16, line.shape[1]))
                rolled = pltpu.roll(wide, 1 + g, axis=1, stride=1, stride_axis=0).astype(bf16)
                for b in range(LAGS):
                    toeplitz[b * B + g : b * B + g + 16, k * B : (k + 1) * B] = rolled[:, (9 - b) * B : (10 - b) * B]
        series = jnp.concatenate([x_ref[b : b + ROWS] for b in range(LAGS)], axis=1).astype(bf16)
        correl = dot(series, toeplitz[...])
        for k in range(K):
            shift = shifts_ref[k, p * per + c]
            whole = lax.div(shift, B)
            rest = shift - whole * B
            moved[k] = pltpu.roll(correl[:, k * B : (k + 1) * B] * scale, lax.rem(B - rest, B), axis=1)
            here, there = moved[k, pl.ds(whole, OUT_ROWS)], moved[k, pl.ds(whole + 1, OUT_ROWS)]
            out_ref[:, k] += jnp.where(lane < B - rest, here, there).reshape(GROUP, PIECE, B)
        return carry

    lax.fori_loop(0, per, channel, 0)


def correlate(rows, tpl, shifts):
    vmem = pl.BlockSpec(memory_space=pltpu.VMEM)
    return pl.pallas_call(
        correlate_kernel,
        out_shape=jax.ShapeDtypeStruct((GROUP, K, PIECE, B), f32),
        in_specs=[vmem, vmem, pl.BlockSpec(memory_space=pltpu.SMEM)],
        out_specs=vmem,
        scratch_shapes=[
            pltpu.VMEM((ALL_ROWS, B), f32),
            pltpu.VMEM((LAGS * B, K * B), bf16),
            pltpu.VMEM((K, ROWS, B), f32),
        ],
        compiler_params=pltpu.CompilerParams(vmem_limit_bytes=32 * 2**20),
    )(rows, tpl, shifts)


def finish_kernel(stack_ref, out_ref, from_group, from_sta, mine, peaks, sems):
    z, p, depth = place()
    s = lax.axis_index("sta")
    in_group = lambda q: {"tm": z * GROUP + q}
    in_depth = lambda w: {"tm": w * GROUP + p}
    in_sta = lambda t: {"sta": t}
    greet(
        [in_group(q) for q in others(p, GROUP)]
        + [in_depth(w) for w in others(z, depth)]
        + [in_sta(t) for t in others(s, K)]
    )

    def stack_copy(owner, q):
        return remote(stack_ref.at[q], from_group.at[owner], sems.at[0, q], sems.at[1, owner], in_group(q))

    def sta_copy(owner, t):
        return remote(mine.at[t], from_sta.at[owner], sems.at[2, t], sems.at[3, owner], in_sta(t))

    def peak_copy(owner, q):
        return remote(peaks.at[0, p], peaks.at[0, owner], sems.at[4, q], sems.at[5, owner], in_group(q))

    def top_copy(owner, w):
        return remote(peaks.at[1, z], peaks.at[1, owner], sems.at[6, w], sems.at[7, owner], in_depth(w))

    for q in others(p, GROUP):
        stack_copy(p, q).start()
    from_group[p] = stack_ref[p]
    for q in others(p, GROUP, -1):
        stack_copy(q, p).wait_recv()
    total = from_group[0]
    for j in range(1, GROUP):
        total += from_group[j]
    mine[...] = total
    for t in others(s, K):
        sta_copy(s, t).start()
    from_sta[s] = mine[s]
    for t in others(s, K, -1):
        sta_copy(t, s).wait_recv()
    stack = from_sta[0]
    for j in range(1, K):
        stack += from_sta[j]
    size = jnp.abs(stack)
    peaks[0, p] = jnp.maximum(size[:8], size[8:])
    for q in others(p, GROUP):
        peak_copy(p, q).start()
    for q in others(p, GROUP, -1):
        peak_copy(q, p).wait_recv()
    peaks[1, z] = jnp.max(peaks[0], axis=0)
    for w in others(z, depth):
        top_copy(z, w).start()
    for w in others(z, depth, -1):
        top_copy(w, z).wait_recv()
    peak = jnp.max(peaks[1])
    out_ref[...] = stack / (peak + 1e-06)
    for q in others(p, GROUP):
        stack_copy(p, q).wait_send()
        peak_copy(p, q).wait_send()
    for t in others(s, K):
        sta_copy(s, t).wait_send()
    for w in others(z, depth):
        top_copy(z, w).wait_send()


def finish(stack):
    vmem = pl.BlockSpec(memory_space=pltpu.VMEM)
    return pl.pallas_call(
        finish_kernel,
        out_shape=jax.ShapeDtypeStruct((PIECE, B), f32),
        in_specs=[vmem],
        out_specs=vmem,
        scratch_shapes=[
            pltpu.VMEM((GROUP, K, PIECE, B), f32),
            pltpu.VMEM((K, PIECE, B), f32),
            pltpu.VMEM((K, PIECE, B), f32),
            pltpu.VMEM((2, GROUP, 8, B), f32),
            pltpu.SemaphoreType.DMA((8, GROUP)),
        ],
        compiler_params=pltpu.CompilerParams(
            collective_id=1, has_side_effects=True, vmem_limit_bytes=16 * 2**20
        ),
    )(stack)


def on_device(data, bank, select, shifts):
    channels = data.shape[0]
    rows, tpl = fetch(select, data.reshape(channels, PIECE, B), bank.reshape(channels, TL // B, B))
    stack = correlate(rows, tpl, shifts)
    return finish(stack).reshape(1, PIECE * B)


def solution(mesh):
    in_specs = (P("sta", "tm"), P("tm", "sta", None), P(), P(None, "sta"))
    out_specs = P("sta", "tm")
    return jax.shard_map(on_device, mesh=mesh, in_specs=in_specs, out_specs=out_specs, check_vma=False)
```

```python
import jax
import jax.numpy as jnp
from jax import lax
from jax.experimental import pallas as pl
from jax.experimental.pallas import tpu as pltpu
from jax.sharding import PartitionSpec as P

TL = 1024
B = 128
TPL_ROWS = TL // B
GROUP = 8
PIECE = 16
OUT_ROWS = GROUP * PIECE
ROWS = OUT_ROWS + 8
ALL_ROWS = ROWS + 8
LAGS = TPL_ROWS + 1
K = 4
MESH = pl.DeviceIdType.MESH
f32, bf16 = jnp.float32, jnp.bfloat16


def dot(a, b):
    return jnp.dot(a, b, preferred_element_type=f32)


def remote(src, dst, sems, device):
    return pltpu.make_async_remote_copy(
        src_ref=src, dst_ref=dst, send_sem=sems.at[0], recv_sem=sems.at[1], device_id=device, device_id_type=MESH
    )


def windows(v):
    ahead, total = v[:, :B], v[:, B:]
    two = total[0:143] + total[1:144]
    four = two[0:141] + two[2:143]
    eight = four[0:136] + four[4:140]
    return eight - ahead[0:136] + ahead[8:144]


def kernel(
    select_hbm, data_hbm, bank_hbm, shifts_hbm, out_ref,
    select_ref, shifts_ref, data_in, bank_in, lay, data_ref, bank_ref, rows_ref, raw, part, got, tpl_ref,
    x_ref, scales, series, toeplitz, moved, stack, from_all, peaks,
    local_sems, bank_sems, data_sems, part_sems, halo_sems, tpl_sems, stack_sems, peak_sems,
):
    me, s = lax.axis_index("tm"), lax.axis_index("sta")
    count = lax.axis_size("tm")
    depth = count // GROUP
    z = lax.div(me, GROUP)
    p = me - z * GROUP
    per = rows_ref.shape[1]
    self = {"tm": me, "sta": s}
    group = [lax.rem(p + i, GROUP) for i in range(1, GROUP)]
    along = [lax.rem(z + i, depth) for i in range(1, depth)]
    in_group = lambda q: {"tm": z * GROUP + q, "sta": s}
    in_depth = lambda w: {"tm": w * GROUP + p, "sta": s}

    barrier = pltpu.get_barrier_semaphore()
    greeted = [in_group(q) for q in group] + [in_depth(w) for w in along]
    greeted += [{"tm": me, "sta": lax.rem(s + i, K)} for i in range(1, K)]
    for device in greeted:
        pl.semaphore_signal(barrier, inc=1, device_id=device, device_id_type=MESH)

    inputs = [(bank_hbm.at[0], bank_in), (data_hbm, data_in), (select_hbm, select_ref), (shifts_hbm, shifts_ref)]
    loads = [pltpu.make_async_copy(src, dst, local_sems.at[i]) for i, (src, dst) in enumerate(inputs)]
    for load in loads:
        load.start()
    channels = data_in.shape[0]
    loads[0].wait()
    for b in range(TPL_ROWS):
        lay[pl.ds(b, channels, stride=TPL_ROWS), :] = bank_in[:, b * B : (b + 1) * B].astype(f32)
    bank_ref[...] = lay[: channels * TPL_ROWS].astype(bf16).reshape(bank_ref.shape)
    loads[1].wait()
    for a in range(PIECE):
        lay[pl.ds(a, channels, stride=PIECE), :] = data_in[:, a * B : (a + 1) * B].astype(f32)
    data_ref[...] = lay[...].astype(bf16).reshape(data_ref.shape)
    loads[2].wait()
    loads[3].wait()
    pl.semaphore_wait(barrier, len(greeted))

    for q in group:
        remote(bank_ref.at[pl.ds(q * per, per)], raw.at[p], bank_sems, in_group(q)).start()
    for q in group:
        remote(data_ref.at[pl.ds(q * per, per)], rows_ref.at[p], data_sems, in_group(q)).start()
    raw[p] = bank_ref[pl.ds(p * per, per)]
    rows_ref[p] = data_ref[pl.ds(p * per, per)]

    bank_all = remote(raw.at[pl.ds(0, GROUP - 1)], raw.at[pl.ds(0, GROUP - 1)], bank_sems, self)
    bank_all.wait_recv()
    for k in range(K):
        wanted = select_ref[k] - z * GROUP
        picked = jnp.zeros(raw.shape[1:], f32)
        for j in range(GROUP):
            picked += jnp.where(wanted == j, raw[j].astype(f32), 0.0)
        picked = picked.astype(bf16)
        for half in range(2):
            part[2 * k + half] = picked[4 * half : 4 * half + 5]
    for w in along:
        remote(part.at[w], got.at[z], part_sems, in_depth(w)).start()
    got[z] = part[z]

    data_all = remote(rows_ref.at[pl.ds(0, GROUP - 1)], rows_ref.at[pl.ds(0, GROUP - 1)], data_sems, self)
    data_all.wait_recv()
    halo = remote(rows_ref.at[0], rows_ref.at[GROUP], halo_sems, in_depth(lax.rem(z + depth - 1, depth)))
    halo.start()

    part_all = remote(got.at[pl.ds(0, depth - 1)], got.at[pl.ds(0, depth - 1)], part_sems, self)
    part_all.wait_recv()
    tpl = got[0].astype(f32)
    for j in range(1, GROUP):
        tpl += got[j].astype(f32)
    mean = jnp.sum(jnp.sum(tpl, axis=2, keepdims=True), axis=1, keepdims=True) / TL
    centred = tpl - mean
    power = jnp.sum(jnp.sum(centred * centred, axis=2, keepdims=True), axis=1, keepdims=True)
    tpl_ref[z] = (centred * lax.rsqrt(power + 1e-05)).astype(bf16)
    for w in along:
        remote(tpl_ref.at[z], tpl_ref.at[z], tpl_sems, in_depth(w)).start()

    halo.wait_recv()
    row = lax.broadcasted_iota(jnp.int32, (ALL_ROWS, B), 0)
    before = lax.broadcasted_iota(jnp.int32, (B, 2 * B), 0) < lax.broadcasted_iota(jnp.int32, (B, 2 * B), 1)
    sums = jnp.where(before, 1.0, 0.0).astype(bf16)
    valid = jnp.where(z == depth - 1, OUT_ROWS, ALL_ROWS)

    def prepare(c, carry):
        x = jnp.where(row < valid, rows_ref[:, c].astype(f32).reshape(ALL_ROWS, B), 0.0)
        x_ref[...] = x
        square = x * x
        high = square.astype(bf16)
        low = (square - high.astype(f32)).astype(bf16)
        window_sum = windows(dot(x.astype(bf16), sums))
        window_sq = windows(dot(high, sums) + dot(low, sums))
        scales[c] = lax.rsqrt(jnp.maximum(window_sq - window_sum * window_sum / TL, TL / 8.0))
        series[c] = jnp.concatenate([x_ref[b : b + ROWS] for b in range(LAGS)], axis=1).astype(bf16)
        return carry

    lax.fori_loop(0, per, prepare, 0)
    stack[...] = jnp.zeros_like(stack)

    lane = lax.broadcasted_iota(jnp.int32, (OUT_ROWS, B), 1)
    flip_at = lax.broadcasted_iota(jnp.int32, (B, B), 0) + lax.broadcasted_iota(jnp.int32, (B, B), 1)
    flip = jnp.where(flip_at == B - 1, 1.0, 0.0).astype(bf16)
    tpl_all = remote(tpl_ref.at[pl.ds(0, depth - 1)], tpl_ref.at[pl.ds(0, depth - 1)], tpl_sems, self)
    tpl_all.wait_recv()

    def correlate(c, carry):
        half = lax.div(c, 5)
        zero = jnp.zeros((1, B), f32)
        for k in range(K):
            tpl = dot(tpl_ref[2 * k + half, c - 4 * half], flip)
            line = jnp.concatenate([zero] + [tpl[7 - m : 8 - m] for m in range(TPL_ROWS)] + [zero], axis=1)
            for g in range(0, B, 16):
                wide = jnp.broadcast_to(line, (16, line.shape[1]))
                rolled = pltpu.roll(wide, 1 + g, axis=1, stride=1, stride_axis=0).astype(bf16)
                for b in range(LAGS):
                    toeplitz[b * B + g : b * B + g + 16, k * B : (k + 1) * B] = rolled[:, (9 - b) * B : (10 - b) * B]
        correl = dot(series[c], toeplitz[...])
        for k in range(K):
            shift = shifts_ref[k, p * per + c]
            whole = jnp.where(shift >= B, 1, 0)
            rest = shift - whole * B
            moved[k] = pltpu.roll(correl[:, k * B : (k + 1) * B] * scales[c], jnp.where(rest == 0, 0, B - rest), axis=1)
            here, there = moved[k, pl.ds(whole, OUT_ROWS)], moved[k, pl.ds(whole + 1, OUT_ROWS)]
            stack[k] += jnp.where(lane < B - rest, here, there).reshape(GROUP, PIECE, B)
        return carry

    lax.fori_loop(0, per, correlate, 0)

    for i in range(GROUP):
        for j in range(K):
            if i + j > 0:
                q, t = lax.rem(p + i, GROUP), lax.rem(s + j, K)
                remote(stack.at[t, q], from_all.at[p * K + s], stack_sems, {"tm": z * GROUP + q, "sta": t}).start()
    from_all[p * K + s] = stack[s, p]
    senders = GROUP * K - 1
    stack_all = remote(from_all.at[pl.ds(0, senders)], from_all.at[pl.ds(0, senders)], stack_sems, self)
    stack_all.wait_recv()
    total = from_all[0]
    for j in range(1, GROUP * K):
        total += from_all[j]
    peaks[pl.ds(me, 1)] = jnp.max(jnp.abs(total), axis=0, keepdims=True)

    def tell(i, carry):
        mine = peaks.at[pl.ds(me, 1)]
        remote(mine, mine, peak_sems, {"tm": lax.rem(me + i, count), "sta": s}).start()
        return carry

    lax.fori_loop(1, count, tell, 0)
    peak_all = remote(peaks.at[pl.ds(0, count - 1)], peaks.at[pl.ds(0, count - 1)], peak_sems, self)
    peak_all.wait_recv()
    out_ref[...] = total / (jnp.max(peaks[...]) + 1e-06)
    for sent in (bank_all, data_all, part_all, halo, tpl_all, stack_all, peak_all):
        sent.wait_send()


def on_device(data, bank, select, shifts):
    channels = data.shape[0]
    per = channels // GROUP
    tpl_parts = (2 * K, 5, TPL_ROWS, B)
    hbm = pl.BlockSpec(memory_space=pltpu.HBM)
    out = pl.pallas_call(
        kernel,
        out_shape=jax.ShapeDtypeStruct((PIECE, B), f32),
        in_specs=[hbm] * 4,
        out_specs=pl.BlockSpec(memory_space=pltpu.VMEM),
        scratch_shapes=[
            pltpu.SMEM(select.shape, jnp.int32),
            pltpu.SMEM(shifts.shape, jnp.int32),
            pltpu.VMEM(data.shape, bf16),
            pltpu.VMEM(bank.shape[1:], bf16),
            pltpu.VMEM((channels * PIECE, B), f32),
            pltpu.VMEM((channels, PIECE, B), bf16),
            pltpu.VMEM((channels, TPL_ROWS, B), bf16),
            pltpu.VMEM((GROUP + 1, per, PIECE, B), bf16),
            pltpu.VMEM((GROUP, per, TPL_ROWS, B), bf16),
            pltpu.VMEM(tpl_parts, bf16),
            pltpu.VMEM(tpl_parts, bf16),
            pltpu.VMEM(tpl_parts, bf16),
            pltpu.VMEM((ALL_ROWS, B), f32),
            pltpu.VMEM((per, ROWS, B), f32),
            pltpu.VMEM((per, ROWS, LAGS * B), bf16),
            pltpu.VMEM((LAGS * B, K * B), bf16),
            pltpu.VMEM((K, ROWS, B), f32),
            pltpu.VMEM((K, GROUP, PIECE, B), f32),
            pltpu.VMEM((GROUP * K, PIECE, B), f32),
            pltpu.VMEM((lax.axis_size("tm"), B), f32),
            pltpu.SemaphoreType.DMA((4,)),
        ]
        + [pltpu.SemaphoreType.DMA((2,))] * 7,
        compiler_params=pltpu.CompilerParams(
            collective_id=0, has_side_effects=True, vmem_limit_bytes=60 * 2**20
        ),
    )(select, data, bank, shifts)
    return out.reshape(1, PIECE * B)


def solution(mesh):
    in_specs = (P("sta", "tm"), P("tm", "sta", None), P(), P(None, "sta"))
    out_specs = P("sta", "tm")
    return jax.shard_map(on_device, mesh=mesh, in_specs=in_specs, out_specs=out_specs, check_vma=False)
```

```python
import jax
import jax.numpy as jnp
from jax import lax
from jax.experimental import pallas as pl
from jax.experimental.pallas import tpu as pltpu
from jax.sharding import PartitionSpec as P

TL = 1024
B = 128
TPL_ROWS = TL // B
GROUP = 8
PIECE = 16
OUT_ROWS = GROUP * PIECE
ROWS = OUT_ROWS + 8
ALL_ROWS = ROWS + 8
LAGS = TPL_ROWS + 1
K = 4
MESH = pl.DeviceIdType.MESH
f32, bf16 = jnp.float32, jnp.bfloat16


def dot(a, b):
    return jnp.dot(a, b, preferred_element_type=f32)


def remote(src, dst, sems, device):
    return pltpu.make_async_remote_copy(
        src_ref=src, dst_ref=dst, send_sem=sems.at[0], recv_sem=sems.at[1], device_id=device, device_id_type=MESH
    )


def hops(step, size):
    return min(step, size - step)


def far_first(depth):
    steps = [(dz, dy, dx) for dz in range(depth) for dy in range(2) for dx in range(4)]
    length = lambda o: hops(o[0], depth) + 2 * o[1] + hops(o[2], 4)
    return sorted(steps, key=length, reverse=True)[:-1]


def windows(v):
    ahead, total = v[:, :B], v[:, B:]
    two = total[0:143] + total[1:144]
    four = two[0:141] + two[2:143]
    eight = four[0:136] + four[4:140]
    return eight - ahead[0:136] + ahead[8:144]


def kernel(
    select_hbm, data_hbm, bank_hbm, shifts_hbm, out_ref,
    select_ref, shifts_ref, data_in, bank_in, lay, data_ref, bank_ref, rows_ref, raw, part, got, tpl_ref,
    x_ref, scales, series, toeplitz, stack, from_all, peaks,
    local_sems, bank_sems, data_sems, part_sems, halo_sems, tpl_sems, stack_sems, peak_sems,
):
    me, s = lax.axis_index("tm"), lax.axis_index("sta")
    count = lax.axis_size("tm")
    depth = count // GROUP
    z = lax.div(me, GROUP)
    p = me - z * GROUP
    per = rows_ref.shape[1]
    self = {"tm": me, "sta": s}
    y, x_at = lax.div(p, 4), lax.rem(p, 4)

    def neighbour(dy, dx):
        return lax.rem(y + dy, 2) * 4 + lax.rem(x_at + dx, 4)

    steps = far_first(depth)
    group = [neighbour(dy, dx) for dz, dy, dx in steps if dz == 0]
    along = [lax.rem(z + dz, depth) for dz, dy, dx in steps if dy == dx == 0]
    in_group = lambda q: {"tm": z * GROUP + q, "sta": s}
    in_depth = lambda w: {"tm": w * GROUP + p, "sta": s}

    barrier = pltpu.get_barrier_semaphore()
    greeted = [in_group(q) for q in group] + [in_depth(w) for w in along]
    greeted += [{"tm": me, "sta": lax.rem(s + i, K)} for i in range(1, K)]
    for device in greeted:
        pl.semaphore_signal(barrier, inc=1, device_id=device, device_id_type=MESH)

    inputs = [(bank_hbm.at[0], bank_in), (data_hbm, data_in), (select_hbm, select_ref), (shifts_hbm, shifts_ref)]
    loads = [pltpu.make_async_copy(src, dst, local_sems.at[i]) for i, (src, dst) in enumerate(inputs)]
    for load in loads:
        load.start()
    channels = data_in.shape[0]
    loads[0].wait()
    for b in range(TPL_ROWS):
        lay[pl.ds(b, channels, stride=TPL_ROWS), :] = bank_in[:, b * B : (b + 1) * B].astype(f32)
    bank_ref[...] = lay[: channels * TPL_ROWS].astype(bf16).reshape(bank_ref.shape)
    loads[1].wait()
    for a in range(PIECE):
        lay[pl.ds(a, channels, stride=PIECE), :] = data_in[:, a * B : (a + 1) * B].astype(f32)
    data_ref[...] = lay[...].astype(bf16).reshape(data_ref.shape)
    loads[2].wait()
    loads[3].wait()
    flip_at = lax.broadcasted_iota(jnp.int32, (B, B), 0) + lax.broadcasted_iota(jnp.int32, (B, B), 1)
    flip = jnp.where(flip_at == B - 1, 1.0, 0.0).astype(bf16)
    pl.semaphore_wait(barrier, len(greeted))

    for q in group:
        remote(bank_ref.at[pl.ds(q * per, per)], raw.at[p], bank_sems, in_group(q)).start()
    for q in group:
        remote(data_ref.at[pl.ds(q * per, per)], rows_ref.at[p], data_sems, in_group(q)).start()
    raw[p] = bank_ref[pl.ds(p * per, per)]
    rows_ref[p] = data_ref[pl.ds(p * per, per)]

    bank_all = remote(raw.at[pl.ds(0, GROUP - 1)], raw.at[pl.ds(0, GROUP - 1)], bank_sems, self)
    bank_all.wait_recv()
    for k in range(K):
        wanted = select_ref[k] - z * GROUP
        here = jnp.where((wanted >= 0) & (wanted < GROUP), 1, 0)
        picked = raw[wanted * here].astype(f32)
        picked = jnp.where(here == 1, picked, 0.0).astype(bf16)
        for half in range(2):
            part[2 * k + half] = picked[4 * half : 4 * half + 5]
    for w in along:
        remote(part.at[w], got.at[z], part_sems, in_depth(w)).start()
    got[z] = part[z]

    data_all = remote(rows_ref.at[pl.ds(0, GROUP - 1)], rows_ref.at[pl.ds(0, GROUP - 1)], data_sems, self)
    data_all.wait_recv()
    halo = remote(rows_ref.at[0], rows_ref.at[GROUP], halo_sems, in_depth(lax.rem(z + depth - 1, depth)))
    halo.start()

    part_all = remote(got.at[pl.ds(0, depth - 1)], got.at[pl.ds(0, depth - 1)], part_sems, self)
    part_all.wait_recv()
    tpl = got[0].astype(f32)
    for j in range(1, GROUP):
        tpl += got[j].astype(f32)
    mean = jnp.sum(jnp.sum(tpl, axis=2, keepdims=True), axis=1, keepdims=True) / TL
    centred = tpl - mean
    power = jnp.sum(jnp.sum(centred * centred, axis=2, keepdims=True), axis=1, keepdims=True)
    normed = (centred * lax.rsqrt(power + 1e-05)).astype(bf16)
    tpl_ref[z] = dot(normed.reshape(5 * TPL_ROWS, B), flip).astype(bf16).reshape(normed.shape)
    for w in along:
        remote(tpl_ref.at[z], tpl_ref.at[z], tpl_sems, in_depth(w)).start()

    halo.wait_recv()
    row = lax.broadcasted_iota(jnp.int32, (ALL_ROWS, B), 0)
    before = lax.broadcasted_iota(jnp.int32, (B, 2 * B), 0) < lax.broadcasted_iota(jnp.int32, (B, 2 * B), 1)
    sums = jnp.where(before, 1.0, 0.0).astype(bf16)
    valid = jnp.where(z == depth - 1, OUT_ROWS, ALL_ROWS)

    def prepare(c, carry):
        x = jnp.where(row < valid, rows_ref[:, c].astype(f32).reshape(ALL_ROWS, B), 0.0)
        x_ref[...] = x
        square = x * x
        high = square.astype(bf16)
        low = (square - high.astype(f32)).astype(bf16)
        window_sum = windows(dot(x.astype(bf16), sums))
        window_sq = windows(dot(high, sums) + dot(low, sums))
        scales[c] = lax.rsqrt(jnp.maximum(window_sq - window_sum * window_sum / TL, TL / 8.0))
        series[c] = jnp.concatenate([x_ref[b : b + ROWS] for b in range(LAGS)], axis=1).astype(bf16)
        return carry

    lax.fori_loop(0, per, prepare, 0)
    stack[...] = jnp.zeros_like(stack)

    lane = lax.broadcasted_iota(jnp.int32, (OUT_ROWS, B), 1)
    tpl_all = remote(tpl_ref.at[pl.ds(0, depth - 1)], tpl_ref.at[pl.ds(0, depth - 1)], tpl_sems, self)
    tpl_all.wait_recv()

    part_row = lax.broadcasted_iota(jnp.int32, (16, B), 0)
    part_lane = lax.broadcasted_iota(jnp.int32, (16, B), 1)
    zero = jnp.zeros((16, B), f32)

    def spread(c, slot):
        half = jnp.where(c >= 5, 1, 0)
        for k in range(K):
            tpl = tpl_ref[2 * k + half, c - 4 * half].astype(f32)
            lines = [jnp.broadcast_to(tpl[m : m + 1], (16, B)) for m in range(TPL_ROWS)]
            for g in range(0, B, 16):
                wraps = part_lane - part_row < 1 + g
                turned = [pltpu.roll(line, 1 + g, axis=1, stride=1, stride_axis=0) for line in lines]
                turned = [zero] + turned + [zero]
                for b in range(LAGS):
                    block = jnp.where(wraps, turned[b + 1], turned[b])
                    toeplitz[slot, b * B + g : b * B + g + 16, k * B : (k + 1) * B] = block.astype(bf16)

    def add(c, slot):
        correl = dot(series[c], toeplitz[slot])
        for k in range(K):
            shift = shifts_ref[k, p * per + c]
            far = shift >= B
            rest = jnp.where(far, shift - B, shift)
            turned = pltpu.roll(correl[:, k * B : (k + 1) * B] * scales[c], jnp.where(rest == 0, 0, B - rest), axis=1)
            first, second, third = turned[:OUT_ROWS], turned[1 : OUT_ROWS + 1], turned[2 : OUT_ROWS + 2]
            near_sum = jnp.where(lane < B - rest, first, second)
            far_sum = jnp.where(lane < B - rest, second, third)
            stack[k] += jnp.where(far, far_sum, near_sum).reshape(GROUP, PIECE, B)

    spread(0, 0)

    def two_channels(i, carry):
        c = 2 * i
        spread(c + 1, 1)
        add(c, 0)
        spread(jnp.minimum(c + 2, per - 1), 0)
        add(c + 1, 1)
        return carry

    lax.fori_loop(0, per // 2, two_channels, 0)
    if per % 2:
        add(per - 1, 0)

    y_lo, core = lax.div(s, 2), lax.rem(s, 2)
    ways = [(dy, dx, dl, dc) for dy in range(2) for dx in range(4) for dl in range(2) for dc in range(2)]
    length = lambda o: (1 if o[2] else 2 * o[0]) + hops(o[1], 4) + 0.1 * o[3]
    for dy, dx, dl, dc in sorted(ways, key=length, reverse=True)[:-1]:
        q, t = neighbour(dy, dx), lax.rem(y_lo + dl, 2) * 2 + lax.rem(core + dc, 2)
        remote(stack.at[t, q], from_all.at[p * K + s], stack_sems, {"tm": z * GROUP + q, "sta": t}).start()
    from_all[p * K + s] = stack[s, p]
    senders = GROUP * K - 1
    stack_all = remote(from_all.at[pl.ds(0, senders)], from_all.at[pl.ds(0, senders)], stack_sems, self)
    stack_all.wait_recv()
    total = from_all[0]
    for j in range(1, GROUP * K):
        total += from_all[j]
    peaks[pl.ds(me, 1)] = jnp.max(jnp.abs(total), axis=0, keepdims=True)

    mine = peaks.at[pl.ds(me, 1)]
    for dz, dy, dx in steps:
        device = {"tm": lax.rem(z + dz, depth) * GROUP + neighbour(dy, dx), "sta": s}
        remote(mine, mine, peak_sems, device).start()
    peak_all = remote(peaks.at[pl.ds(0, count - 1)], peaks.at[pl.ds(0, count - 1)], peak_sems, self)
    peak_all.wait_recv()
    out_ref[...] = total / (jnp.max(peaks[...]) + 1e-06)
    for sent in (bank_all, data_all, part_all, halo, tpl_all, stack_all, peak_all):
        sent.wait_send()


def on_device(data, bank, select, shifts):
    channels = data.shape[0]
    per = channels // GROUP
    tpl_parts = (2 * K, 5, TPL_ROWS, B)
    hbm = pl.BlockSpec(memory_space=pltpu.HBM)
    out = pl.pallas_call(
        kernel,
        out_shape=jax.ShapeDtypeStruct((PIECE, B), f32),
        in_specs=[hbm] * 4,
        out_specs=pl.BlockSpec(memory_space=pltpu.VMEM),
        scratch_shapes=[
            pltpu.SMEM(select.shape, jnp.int32),
            pltpu.SMEM(shifts.shape, jnp.int32),
            pltpu.VMEM(data.shape, bf16),
            pltpu.VMEM(bank.shape[1:], bf16),
            pltpu.VMEM((channels * PIECE, B), f32),
            pltpu.VMEM((channels, PIECE, B), bf16),
            pltpu.VMEM((channels, TPL_ROWS, B), bf16),
            pltpu.VMEM((GROUP + 1, per, PIECE, B), bf16),
            pltpu.VMEM((GROUP, per, TPL_ROWS, B), bf16),
            pltpu.VMEM(tpl_parts, bf16),
            pltpu.VMEM(tpl_parts, bf16),
            pltpu.VMEM(tpl_parts, bf16),
            pltpu.VMEM((ALL_ROWS, B), f32),
            pltpu.VMEM((per, ROWS, B), f32),
            pltpu.VMEM((per, ROWS, LAGS * B), bf16),
            pltpu.VMEM((2, LAGS * B, K * B), bf16),
            pltpu.VMEM((K, GROUP, PIECE, B), f32),
            pltpu.VMEM((GROUP * K, PIECE, B), f32),
            pltpu.VMEM((lax.axis_size("tm"), B), f32),
            pltpu.SemaphoreType.DMA((4,)),
        ]
        + [pltpu.SemaphoreType.DMA((2,))] * 7,
        compiler_params=pltpu.CompilerParams(
            collective_id=0, has_side_effects=True, vmem_limit_bytes=60 * 2**20
        ),
    )(select, data, bank, shifts)
    return out.reshape(1, PIECE * B)


def solution(mesh):
    in_specs = (P("sta", "tm"), P("tm", "sta", None), P(), P(None, "sta"))
    out_specs = P("sta", "tm")
    return jax.shard_map(on_device, mesh=mesh, in_specs=in_specs, out_specs=out_specs, check_vma=False)
```

```python
import jax
import jax.numpy as jnp
from jax import lax
from jax.experimental import pallas as pl
from jax.experimental.pallas import tpu as pltpu
from jax.sharding import PartitionSpec as P

TL = 1024
B = 128
TPL_ROWS = TL // B
GROUP = 8
PIECE = 16
OUT_ROWS = GROUP * PIECE
ROWS = OUT_ROWS + 8
ALL_ROWS = ROWS + 8
LAGS = TPL_ROWS + 1
K = 4
MESH = pl.DeviceIdType.MESH
f32, bf16 = jnp.float32, jnp.bfloat16


def dot(a, b):
    return jnp.dot(a, b, preferred_element_type=f32)


def remote(src, dst, sems, device):
    return pltpu.make_async_remote_copy(
        src_ref=src, dst_ref=dst, send_sem=sems.at[0], recv_sem=sems.at[1], device_id=device, device_id_type=MESH
    )


def hops(step, size):
    return min(step, size - step)


def far_first(depth):
    steps = [(dz, dy, dx) for dz in range(depth) for dy in range(2) for dx in range(4)]
    length = lambda o: hops(o[0], depth) + 2 * o[1] + hops(o[2], 4)
    return sorted(steps, key=length, reverse=True)[:-1]


def windows(v):
    ahead, total = v[:, :B], v[:, B:]
    two = total[0:143] + total[1:144]
    four = two[0:141] + two[2:143]
    eight = four[0:136] + four[4:140]
    return eight - ahead[0:136] + ahead[8:144]


def kernel(
    select_hbm, data_hbm, bank_hbm, shifts_hbm, out_ref,
    select_ref, shifts_ref, data_in, bank_in, lay, data_ref, bank_ref, rows_ref, raw, part, got, tpl_ref,
    x_ref, scales, series, toeplitz, stack, from_all, peaks,
    local_sems, bank_sems, data_sems, part_sems, halo_sems, stack_sems, peak_sems, tpl_sent, tpl_come,
):
    me, s = lax.axis_index("tm"), lax.axis_index("sta")
    count = lax.axis_size("tm")
    depth = count // GROUP
    z = lax.div(me, GROUP)
    p = me - z * GROUP
    per = rows_ref.shape[1]
    self = {"tm": me, "sta": s}
    y, x_at = lax.div(p, 4), lax.rem(p, 4)

    def neighbour(dy, dx):
        return lax.rem(y + dy, 2) * 4 + lax.rem(x_at + dx, 4)

    steps = far_first(depth)
    group = [neighbour(dy, dx) for dz, dy, dx in steps if dz == 0]
    along = [lax.rem(z + dz, depth) for dz, dy, dx in steps if dy == dx == 0]
    in_group = lambda q: {"tm": z * GROUP + q, "sta": s}
    in_depth = lambda w: {"tm": w * GROUP + p, "sta": s}

    def tpl_copy(w, device):
        return pltpu.make_async_remote_copy(
            src_ref=tpl_ref.at[w], dst_ref=tpl_ref.at[w], send_sem=tpl_sent, recv_sem=tpl_come.at[w],
            device_id=device, device_id_type=MESH,
        )

    barrier = pltpu.get_barrier_semaphore()
    greeted = [in_group(q) for q in group] + [in_depth(w) for w in along]
    greeted += [{"tm": me, "sta": lax.rem(s + i, K)} for i in range(1, K)]
    for device in greeted:
        pl.semaphore_signal(barrier, inc=1, device_id=device, device_id_type=MESH)

    inputs = [(bank_hbm.at[0], bank_in), (data_hbm, data_in), (select_hbm, select_ref), (shifts_hbm, shifts_ref)]
    loads = [pltpu.make_async_copy(src, dst, local_sems.at[i]) for i, (src, dst) in enumerate(inputs)]
    for load in loads:
        load.start()
    channels = data_in.shape[0]
    flip_at = lax.broadcasted_iota(jnp.int32, (B, B), 0) + lax.broadcasted_iota(jnp.int32, (B, B), 1)
    flip = jnp.where(flip_at == B - 1, 1.0, 0.0).astype(bf16)
    loads[0].wait()
    rows = bank_in[...].astype(f32)
    centred = rows - jnp.sum(rows, axis=1, keepdims=True) / TL
    power = jnp.sum(centred * centred, axis=1, keepdims=True)
    normed = (centred * lax.rsqrt(power + 1e-05)).astype(bf16)
    for b in range(TPL_ROWS):
        lay[pl.ds(b, channels, stride=TPL_ROWS), :] = dot(normed[:, b * B : (b + 1) * B], flip)
    bank_ref[...] = lay[: channels * TPL_ROWS].astype(bf16).reshape(bank_ref.shape)
    loads[1].wait()
    for a in range(PIECE):
        lay[pl.ds(a, channels, stride=PIECE), :] = data_in[:, a * B : (a + 1) * B].astype(f32)
    data_ref[...] = lay[...].astype(bf16).reshape(data_ref.shape)
    loads[2].wait()
    loads[3].wait()
    pl.semaphore_wait(barrier, len(greeted))

    for q in group:
        remote(bank_ref.at[pl.ds(q * per, per)], raw.at[p], bank_sems, in_group(q)).start()
    for q in group:
        remote(data_ref.at[pl.ds(q * per, per)], rows_ref.at[p], data_sems, in_group(q)).start()
    raw[p] = bank_ref[pl.ds(p * per, per)]
    rows_ref[p] = data_ref[pl.ds(p * per, per)]

    bank_all = remote(raw.at[pl.ds(0, GROUP - 1)], raw.at[pl.ds(0, GROUP - 1)], bank_sems, self)
    bank_all.wait_recv()
    for k in range(K):
        offered = raw[lax.rem(select_ref[k], GROUP)]
        part[2 * k] = offered[:5]
        part[2 * k + 1] = offered[4:]
    for w in along:
        remote(part.at[w], got.at[z], part_sems, in_depth(w)).start()
    got[z] = part[z]

    data_all = remote(rows_ref.at[pl.ds(0, GROUP - 1)], rows_ref.at[pl.ds(0, GROUP - 1)], data_sems, self)
    data_all.wait_recv()
    halo = remote(rows_ref.at[0], rows_ref.at[GROUP], halo_sems, in_depth(lax.rem(z + depth - 1, depth)))
    halo.start()

    part_all = remote(got.at[pl.ds(0, depth - 1)], got.at[pl.ds(0, depth - 1)], part_sems, self)
    part_all.wait_recv()
    tpl_ref[z] = got[lax.div(select_ref[lax.div(z, 2)], GROUP)]
    for w in along:
        tpl_copy(z, in_depth(w)).start()

    part_row = lax.broadcasted_iota(jnp.int32, (16, B), 0)
    part_lane = lax.broadcasted_iota(jnp.int32, (16, B), 1)
    zero = jnp.zeros((16, B), f32)

    def spread_one(tpl, c, k):
        tpl = tpl.astype(f32)
        lines = [jnp.broadcast_to(tpl[m : m + 1], (16, B)) for m in range(TPL_ROWS)]
        for g in range(0, B, 16):
            wraps = part_lane - part_row < 1 + g
            turned = [pltpu.roll(line, 1 + g, axis=1, stride=1, stride_axis=0) for line in lines]
            turned = [zero] + turned + [zero]
            for b in range(LAGS):
                block = jnp.where(wraps, turned[b + 1], turned[b])
                toeplitz[c, k, b * B + g : b * B + g + 16] = block.astype(bf16)

    def spread(w):
        k = lax.div(w, 2)
        half = w - 2 * k
        for i in range(4):
            spread_one(tpl_ref[w, i + half], 5 * half + i, k)

        @pl.when(half == 0)
        def _():
            spread_one(tpl_ref[w, 4], 4, k)

    spread(z)

    halo.wait_recv()
    row = lax.broadcasted_iota(jnp.int32, (ALL_ROWS, B), 0)
    before = lax.broadcasted_iota(jnp.int32, (B, 2 * B), 0) < lax.broadcasted_iota(jnp.int32, (B, 2 * B), 1)
    sums = jnp.where(before, 1.0, 0.0).astype(bf16)
    valid = jnp.where(z == depth - 1, OUT_ROWS, ALL_ROWS)

    def prepare(c, carry):
        x = jnp.where(row < valid, rows_ref[:, c].astype(f32).reshape(ALL_ROWS, B), 0.0)
        x_ref[...] = x
        square = x * x
        high = square.astype(bf16)
        low = (square - high.astype(f32)).astype(bf16)
        window_sum = windows(dot(x.astype(bf16), sums))
        window_sq = windows(dot(high, sums) + dot(low, sums))
        scales[c] = lax.rsqrt(jnp.maximum(window_sq - window_sum * window_sum / TL, TL / 8.0))
        series[c] = jnp.concatenate([x_ref[b : b + ROWS] for b in range(LAGS)], axis=1).astype(bf16)
        return carry

    lax.fori_loop(0, per, prepare, 0)
    stack[...] = jnp.zeros_like(stack)

    lane = lax.broadcasted_iota(jnp.int32, (OUT_ROWS, B), 1)

    def arrive(i, carry):
        away = jnp.where(lax.rem(i, 2) == 1, lax.div(i + 1, 2), depth - lax.div(i, 2))
        w = lax.rem(z + away, depth)
        tpl_copy(w, self).wait_recv()
        spread(w)
        return carry

    lax.fori_loop(1, depth, arrive, 0)

    def correlate(c):
        return dot(series[c], jnp.concatenate([toeplitz[c, k] for k in range(K)], axis=1))

    def add(c, k, correl):
        shift = shifts_ref[k, p * per + c]
        far = shift >= B
        rest = jnp.where(far, shift - B, shift)
        turned = pltpu.roll(correl[:, k * B : (k + 1) * B] * scales[c], jnp.where(rest == 0, 0, B - rest), axis=1)
        first, second, third = turned[:OUT_ROWS], turned[1 : OUT_ROWS + 1], turned[2 : OUT_ROWS + 2]
        near_sum = jnp.where(lane < B - rest, first, second)
        far_sum = jnp.where(lane < B - rest, second, third)
        stack[k] += jnp.where(far, far_sum, near_sum).reshape(GROUP, PIECE, B)

    def channel(c, carry):
        correl = correlate(c)
        for k in range(K):
            add(c, k, correl)
        return carry

    lax.fori_loop(0, per - 1, channel, 0, unroll=4)

    correl = correlate(per - 1)
    for k in range(K):
        add(per - 1, k, correl)
        for dz, dy, dx in steps:
            if dz == 0:
                q = neighbour(dy, dx)
                remote(stack.at[k, q], from_all.at[p * K + s], stack_sems, {"tm": z * GROUP + q, "sta": k}).start()

        @pl.when(s != k)
        def _():
            remote(stack.at[k, p], from_all.at[p * K + s], stack_sems, {"tm": me, "sta": k}).start()

    from_all[p * K + s] = stack[s, p]
    senders = GROUP * K - 1
    stack_all = remote(from_all.at[pl.ds(0, senders)], from_all.at[pl.ds(0, senders)], stack_sems, self)
    stack_all.wait_recv()
    total = from_all[0]
    for j in range(1, GROUP * K):
        total += from_all[j]
    peaks[pl.ds(me, 1)] = jnp.max(jnp.abs(total), axis=0, keepdims=True)

    mine = peaks.at[pl.ds(me, 1)]
    for dz, dy, dx in steps:
        device = {"tm": lax.rem(z + dz, depth) * GROUP + neighbour(dy, dx), "sta": s}
        remote(mine, mine, peak_sems, device).start()
    peak_all = remote(peaks.at[pl.ds(0, count - 1)], peaks.at[pl.ds(0, count - 1)], peak_sems, self)
    peak_all.wait_recv()
    out_ref[...] = total / (jnp.max(peaks[...]) + 1e-06)
    tpl_all = pltpu.make_async_copy(tpl_ref.at[pl.ds(0, depth - 1)], tpl_ref.at[pl.ds(0, depth - 1)], tpl_sent)
    tpl_all.wait()
    for sent in (bank_all, data_all, part_all, halo, stack_all, peak_all):
        sent.wait_send()


def on_device(data, bank, select, shifts):
    channels = data.shape[0]
    per = channels // GROUP
    tpl_parts = (2 * K, 5, TPL_ROWS, B)
    hbm = pl.BlockSpec(memory_space=pltpu.HBM)
    out = pl.pallas_call(
        kernel,
        out_shape=jax.ShapeDtypeStruct((PIECE, B), f32),
        in_specs=[hbm] * 4,
        out_specs=pl.BlockSpec(memory_space=pltpu.VMEM),
        scratch_shapes=[
            pltpu.SMEM(select.shape, jnp.int32),
            pltpu.SMEM(shifts.shape, jnp.int32),
            pltpu.VMEM(data.shape, bf16),
            pltpu.VMEM(bank.shape[1:], bf16),
            pltpu.VMEM((channels * PIECE, B), f32),
            pltpu.VMEM((channels, PIECE, B), bf16),
            pltpu.VMEM((channels, TPL_ROWS, B), bf16),
            pltpu.VMEM((GROUP + 1, per, PIECE, B), bf16),
            pltpu.VMEM((GROUP, per, TPL_ROWS, B), bf16),
            pltpu.VMEM(tpl_parts, bf16),
            pltpu.VMEM(tpl_parts, bf16),
            pltpu.VMEM(tpl_parts, bf16),
            pltpu.VMEM((ALL_ROWS, B), f32),
            pltpu.VMEM((per, ROWS, B), f32),
            pltpu.VMEM((per, ROWS, LAGS * B), bf16),
            pltpu.VMEM((per, K, LAGS * B, B), bf16),
            pltpu.VMEM((K, GROUP, PIECE, B), f32),
            pltpu.VMEM((GROUP * K, PIECE, B), f32),
            pltpu.VMEM((lax.axis_size("tm"), B), f32),
            pltpu.SemaphoreType.DMA((4,)),
        ]
        + [pltpu.SemaphoreType.DMA((2,))] * 6
        + [pltpu.SemaphoreType.DMA, pltpu.SemaphoreType.DMA((2 * K,))],
        compiler_params=pltpu.CompilerParams(
            collective_id=0, has_side_effects=True, vmem_limit_bytes=60 * 2**20
        ),
    )(select, data, bank, shifts)
    return out.reshape(1, PIECE * B)


def solution(mesh):
    in_specs = (P("sta", "tm"), P("tm", "sta", None), P(), P(None, "sta"))
    out_specs = P("sta", "tm")
    return jax.shard_map(on_device, mesh=mesh, in_specs=in_specs, out_specs=out_specs, check_vma=False)
```

```python
import jax
import jax.numpy as jnp
from jax import lax
from jax.experimental import pallas as pl
from jax.experimental.pallas import tpu as pltpu
from jax.sharding import PartitionSpec as P

TL = 1024
B = 128
TPL_ROWS = TL // B
GROUP = 8
PIECE = 16
OUT_ROWS = GROUP * PIECE
ROWS = OUT_ROWS + 8
ALL_ROWS = ROWS + 8
LAGS = TPL_ROWS + 1
K = 4
MESH = pl.DeviceIdType.MESH
f32, bf16 = jnp.float32, jnp.bfloat16


def dot(a, b):
    return jnp.dot(a, b, preferred_element_type=f32)


def remote(src, dst, sems, device):
    return pltpu.make_async_remote_copy(
        src_ref=src, dst_ref=dst, send_sem=sems.at[0], recv_sem=sems.at[1], device_id=device, device_id_type=MESH
    )


def hops(step, size):
    return min(step, size - step)


def far_first(depth):
    steps = [(dz, dy, dx) for dz in range(depth) for dy in range(2) for dx in range(4)]
    length = lambda o: hops(o[0], depth) + 2 * o[1] + hops(o[2], 4)
    return sorted(steps, key=length, reverse=True)[:-1]


def windows(v):
    ahead, total = v[:, :B], v[:, B:]
    two = total[0:143] + total[1:144]
    four = two[0:141] + two[2:143]
    eight = four[0:136] + four[4:140]
    return eight - ahead[0:136] + ahead[8:144]


def kernel(
    select_hbm, data_hbm, bank_hbm, shifts_hbm, out_ref,
    select_ref, shifts_ref, data_in, bank_in, lay, data_ref, bank_ref, rows_ref, raw, part, got, tpl_ref,
    x_ref, scales, series, toeplitz, stack, from_all, peaks,
    local_sems, bank_sems, data_sems, part_sems, halo_sems, stack_sems, peak_sems, tpl_sent, tpl_come,
):
    me, s = lax.axis_index("tm"), lax.axis_index("sta")
    count = lax.axis_size("tm")
    depth = count // GROUP
    z = lax.div(me, GROUP)
    p = me - z * GROUP
    per = rows_ref.shape[1]
    self = {"tm": me, "sta": s}
    y, x_at = lax.div(p, 4), lax.rem(p, 4)

    def neighbour(dy, dx):
        return lax.rem(y + dy, 2) * 4 + lax.rem(x_at + dx, 4)

    steps = far_first(depth)
    group = [neighbour(dy, dx) for dz, dy, dx in steps if dz == 0]
    along = [lax.rem(z + dz, depth) for dz, dy, dx in steps if dy == dx == 0]
    in_group = lambda q: {"tm": z * GROUP + q, "sta": s}
    in_depth = lambda w: {"tm": w * GROUP + p, "sta": s}

    def tpl_copy(w, device):
        return pltpu.make_async_remote_copy(
            src_ref=tpl_ref.at[w], dst_ref=tpl_ref.at[w], send_sem=tpl_sent, recv_sem=tpl_come.at[w],
            device_id=device, device_id_type=MESH,
        )

    inputs = [(bank_hbm.at[0], bank_in), (data_hbm, data_in), (select_hbm, select_ref), (shifts_hbm, shifts_ref)]
    loads = [pltpu.make_async_copy(src, dst, local_sems.at[i]) for i, (src, dst) in enumerate(inputs)]
    for load in loads:
        load.start()
    barrier = pltpu.get_barrier_semaphore()
    greeted = [in_depth(w) for w in along] + [in_group(q) for q in group]
    greeted += [{"tm": me, "sta": lax.rem(s + i, K)} for i in range(1, K)]
    for device in greeted:
        pl.semaphore_signal(barrier, inc=1, device_id=device, device_id_type=MESH)

    channels = data_in.shape[0]
    flip_at = lax.broadcasted_iota(jnp.int32, (B, B), 0) + lax.broadcasted_iota(jnp.int32, (B, B), 1)
    flip = jnp.where(flip_at == B - 1, 1.0, 0.0).astype(bf16)
    loads[0].wait()
    rows = bank_in[...].astype(f32)
    centred = rows - jnp.sum(rows, axis=1, keepdims=True) / TL
    power = jnp.sum(centred * centred, axis=1, keepdims=True)
    normed = (centred * lax.rsqrt(power + 1e-05)).astype(bf16)
    for b in range(TPL_ROWS):
        lay[pl.ds(b, channels, stride=TPL_ROWS), :] = dot(normed[:, b * B : (b + 1) * B], flip)
    bank_ref[...] = lay[: channels * TPL_ROWS].astype(bf16).reshape(bank_ref.shape)
    pl.semaphore_wait(barrier, len(greeted))

    for q in group:
        remote(bank_ref.at[pl.ds(q * per, per)], raw.at[p], bank_sems, in_group(q)).start()
    loads[1].wait()
    for a in range(PIECE):
        lay[pl.ds(a, channels, stride=PIECE), :] = data_in[:, a * B : (a + 1) * B].astype(f32)
    data_ref[...] = lay[...].astype(bf16).reshape(data_ref.shape)
    for q in group[::-1]:
        remote(data_ref.at[pl.ds(q * per, per)], rows_ref.at[p], data_sems, in_group(q)).start()
    raw[p] = bank_ref[pl.ds(p * per, per)]
    rows_ref[p] = data_ref[pl.ds(p * per, per)]

    loads[2].wait()
    loads[3].wait()
    bank_all = remote(raw.at[pl.ds(0, GROUP - 1)], raw.at[pl.ds(0, GROUP - 1)], bank_sems, self)
    bank_all.wait_recv()
    for k in range(K):
        offered = raw[lax.rem(select_ref[k], GROUP)]
        part[2 * k] = offered[:5]
        part[2 * k + 1] = offered[4:]
    for w in along:
        remote(part.at[w], got.at[z], part_sems, in_depth(w)).start()
    got[z] = part[z]

    data_all = remote(rows_ref.at[pl.ds(0, GROUP - 1)], rows_ref.at[pl.ds(0, GROUP - 1)], data_sems, self)
    data_all.wait_recv()
    halo = remote(rows_ref.at[0], rows_ref.at[GROUP], halo_sems, in_depth(lax.rem(z + depth - 1, depth)))
    halo.start()

    part_all = remote(got.at[pl.ds(0, depth - 1)], got.at[pl.ds(0, depth - 1)], part_sems, self)
    part_all.wait_recv()
    tpl_ref[z] = got[lax.div(select_ref[lax.div(z, 2)], GROUP)]
    for w in along:
        tpl_copy(z, in_depth(w)).start()

    part_row = lax.broadcasted_iota(jnp.int32, (16, B), 0)
    part_lane = lax.broadcasted_iota(jnp.int32, (16, B), 1)
    zero = jnp.zeros((16, B), f32)

    def spread_one(tpl, c, k):
        tpl = tpl.astype(f32)
        lines = [jnp.broadcast_to(tpl[m : m + 1], (16, B)) for m in range(TPL_ROWS)]
        for g in range(0, B, 16):
            wraps = part_lane - part_row < 1 + g
            turned = [pltpu.roll(line, 1 + g, axis=1, stride=1, stride_axis=0) for line in lines]
            turned = [zero] + turned + [zero]
            for b in range(LAGS):
                block = jnp.where(wraps, turned[b + 1], turned[b])
                toeplitz[c, k, b * B + g : b * B + g + 16] = block.astype(bf16)

    def spread(w):
        k = lax.div(w, 2)
        half = w - 2 * k
        for i in range(4):
            spread_one(tpl_ref[w, i + half], 5 * half + i, k)

        @pl.when(half == 0)
        def _():
            spread_one(tpl_ref[w, 4], 4, k)

    spread(z)

    halo.wait_recv()
    row = lax.broadcasted_iota(jnp.int32, (ALL_ROWS, B), 0)
    before = lax.broadcasted_iota(jnp.int32, (B, 2 * B), 0) < lax.broadcasted_iota(jnp.int32, (B, 2 * B), 1)
    sums = jnp.where(before, 1.0, 0.0).astype(bf16)
    valid = jnp.where(z == depth - 1, OUT_ROWS, ALL_ROWS)

    def prepare(c, carry):
        x = jnp.where(row < valid, rows_ref[:, c].astype(f32).reshape(ALL_ROWS, B), 0.0)
        x_ref[...] = x
        square = x * x
        high = square.astype(bf16)
        low = (square - high.astype(f32)).astype(bf16)
        window_sum = windows(dot(x.astype(bf16), sums))
        window_sq = windows(dot(high, sums) + dot(low, sums))
        scales[c] = lax.rsqrt(jnp.maximum(window_sq - window_sum * window_sum / TL, TL / 8.0))
        series[c] = jnp.concatenate([x_ref[b : b + ROWS] for b in range(LAGS)], axis=1).astype(bf16)
        return carry

    lax.fori_loop(0, per, prepare, 0)
    stack[...] = jnp.zeros_like(stack)

    lane = lax.broadcasted_iota(jnp.int32, (OUT_ROWS, B), 1)

    def arrive(i, carry):
        away = jnp.where(lax.rem(i, 2) == 1, lax.div(i + 1, 2), depth - lax.div(i, 2))
        w = lax.rem(z + away, depth)
        tpl_copy(w, self).wait_recv()
        spread(w)
        return carry

    lax.fori_loop(1, depth, arrive, 0)

    def correlate(c):
        return dot(series[c], jnp.concatenate([toeplitz[c, k] for k in range(K)], axis=1))

    def add(c, k, correl):
        shift = shifts_ref[k, p * per + c]
        far = shift >= B
        rest = jnp.where(far, shift - B, shift)
        turned = pltpu.roll(correl[:, k * B : (k + 1) * B] * scales[c], jnp.where(rest == 0, 0, B - rest), axis=1)
        first, second, third = turned[:OUT_ROWS], turned[1 : OUT_ROWS + 1], turned[2 : OUT_ROWS + 2]
        near_sum = jnp.where(lane < B - rest, first, second)
        far_sum = jnp.where(lane < B - rest, second, third)
        stack[k] += jnp.where(far, far_sum, near_sum).reshape(GROUP, PIECE, B)

    def channel(c, carry):
        correl = correlate(c)
        for k in range(K):
            add(c, k, correl)
        return carry

    lax.fori_loop(0, per - 1, channel, 0, unroll=True)

    correl = correlate(per - 1)
    for k in range(K):
        add(per - 1, k, correl)
        for dz, dy, dx in steps:
            if dz == 0:
                q = neighbour(dy, dx)
                remote(stack.at[k, q], from_all.at[p * K + s], stack_sems, {"tm": z * GROUP + q, "sta": k}).start()

        @pl.when(s != k)
        def _():
            remote(stack.at[k, p], from_all.at[p * K + s], stack_sems, {"tm": me, "sta": k}).start()

    from_all[p * K + s] = stack[s, p]
    senders = GROUP * K - 1
    stack_all = remote(from_all.at[pl.ds(0, senders)], from_all.at[pl.ds(0, senders)], stack_sems, self)
    stack_all.wait_recv()
    total = from_all[0]
    for j in range(1, GROUP * K):
        total += from_all[j]
    peaks[pl.ds(me, 1)] = jnp.max(jnp.abs(total), axis=0, keepdims=True)

    mine = peaks.at[pl.ds(me, 1)]
    for dz, dy, dx in steps:
        device = {"tm": lax.rem(z + dz, depth) * GROUP + neighbour(dy, dx), "sta": s}
        remote(mine, mine, peak_sems, device).start()
    peak_all = remote(peaks.at[pl.ds(0, count - 1)], peaks.at[pl.ds(0, count - 1)], peak_sems, self)
    peak_all.wait_recv()
    out_ref[...] = total / (jnp.max(peaks[...]) + 1e-06)
    tpl_all = pltpu.make_async_copy(tpl_ref.at[pl.ds(0, depth - 1)], tpl_ref.at[pl.ds(0, depth - 1)], tpl_sent)
    tpl_all.wait()
    for sent in (bank_all, data_all, part_all, halo, stack_all, peak_all):
        sent.wait_send()


def on_device(data, bank, select, shifts):
    channels = data.shape[0]
    per = channels // GROUP
    tpl_parts = (2 * K, 5, TPL_ROWS, B)
    hbm = pl.BlockSpec(memory_space=pltpu.HBM)
    out = pl.pallas_call(
        kernel,
        out_shape=jax.ShapeDtypeStruct((PIECE, B), f32),
        in_specs=[hbm] * 4,
        out_specs=pl.BlockSpec(memory_space=pltpu.VMEM),
        scratch_shapes=[
            pltpu.SMEM(select.shape, jnp.int32),
            pltpu.SMEM(shifts.shape, jnp.int32),
            pltpu.VMEM(data.shape, bf16),
            pltpu.VMEM(bank.shape[1:], bf16),
            pltpu.VMEM((channels * PIECE, B), f32),
            pltpu.VMEM((channels, PIECE, B), bf16),
            pltpu.VMEM((channels, TPL_ROWS, B), bf16),
            pltpu.VMEM((GROUP + 1, per, PIECE, B), bf16),
            pltpu.VMEM((GROUP, per, TPL_ROWS, B), bf16),
            pltpu.VMEM(tpl_parts, bf16),
            pltpu.VMEM(tpl_parts, bf16),
            pltpu.VMEM(tpl_parts, bf16),
            pltpu.VMEM((ALL_ROWS, B), f32),
            pltpu.VMEM((per, ROWS, B), f32),
            pltpu.VMEM((per, ROWS, LAGS * B), bf16),
            pltpu.VMEM((per, K, LAGS * B, B), bf16),
            pltpu.VMEM((K, GROUP, PIECE, B), f32),
            pltpu.VMEM((GROUP * K, PIECE, B), f32),
            pltpu.VMEM((lax.axis_size("tm"), B), f32),
            pltpu.SemaphoreType.DMA((4,)),
        ]
        + [pltpu.SemaphoreType.DMA((2,))] * 6
        + [pltpu.SemaphoreType.DMA, pltpu.SemaphoreType.DMA((2 * K,))],
        compiler_params=pltpu.CompilerParams(
            collective_id=0, has_side_effects=True, vmem_limit_bytes=60 * 2**20
        ),
    )(select, data, bank, shifts)
    return out.reshape(1, PIECE * B)


def solution(mesh):
    in_specs = (P("sta", "tm"), P("tm", "sta", None), P(), P(None, "sta"))
    out_specs = P("sta", "tm")
    return jax.shard_map(on_device, mesh=mesh, in_specs=in_specs, out_specs=out_specs, check_vma=False)
```

```python
import jax
import jax.numpy as jnp
from jax import lax
from jax.experimental import pallas as pl
from jax.experimental.pallas import tpu as pltpu
from jax.sharding import PartitionSpec as P

TL = 1024
B = 128
TPL_ROWS = TL // B
GROUP = 8
PIECE = 16
OUT_ROWS = GROUP * PIECE
ROWS = OUT_ROWS + 8
ALL_ROWS = ROWS + 8
LAGS = TPL_ROWS + 1
K = 4
MESH = pl.DeviceIdType.MESH
f32, bf16 = jnp.float32, jnp.bfloat16


def dot(a, b):
    return jnp.dot(a, b, preferred_element_type=f32)


def remote(src, dst, sems, device):
    return pltpu.make_async_remote_copy(
        src_ref=src, dst_ref=dst, send_sem=sems.at[0], recv_sem=sems.at[1], device_id=device, device_id_type=MESH
    )


def hops(step, size):
    return min(step, size - step)


def far_first(depth):
    steps = [(dz, dy, dx) for dz in range(depth) for dy in range(2) for dx in range(4)]
    length = lambda o: hops(o[0], depth) + 2 * o[1] + hops(o[2], 4)
    return sorted(steps, key=length, reverse=True)[:-1]


def windows(v):
    ahead, total = v[:, :B], v[:, B:]
    two = total[0:143] + total[1:144]
    four = two[0:141] + two[2:143]
    eight = four[0:136] + four[4:140]
    return eight - ahead[0:136] + ahead[8:144]


def kernel(
    select_hbm, data_hbm, bank_hbm, shifts_hbm, out_ref,
    select_ref, shifts_ref, data_in, bank_in, lay, data_ref, bank_ref, rows_ref, raw, part, got, tpl_ref,
    x_ref, scales, series, toeplitz, stack, from_all, peaks,
    local_sems, bank_sems, data_sems, part_sems, halo_sems, stack_sems, peak_sems, tpl_sent, tpl_come,
):
    me, s = lax.axis_index("tm"), lax.axis_index("sta")
    count = lax.axis_size("tm")
    depth = count // GROUP
    z = lax.div(me, GROUP)
    p = me - z * GROUP
    per = rows_ref.shape[1]
    self = {"tm": me, "sta": s}
    y, x_at = lax.div(p, 4), lax.rem(p, 4)

    def neighbour(dy, dx):
        return lax.rem(y + dy, 2) * 4 + lax.rem(x_at + dx, 4)

    steps = far_first(depth)
    group = [neighbour(dy, dx) for dz, dy, dx in steps if dz == 0]
    along = [lax.rem(z + dz, depth) for dz, dy, dx in steps if dy == dx == 0]
    in_group = lambda q: {"tm": z * GROUP + q, "sta": s}
    in_depth = lambda w: {"tm": w * GROUP + p, "sta": s}

    def tpl_copy(w, device):
        return pltpu.make_async_remote_copy(
            src_ref=tpl_ref.at[w], dst_ref=tpl_ref.at[w], send_sem=tpl_sent, recv_sem=tpl_come.at[w],
            device_id=device, device_id_type=MESH,
        )

    inputs = [(bank_hbm.at[0], bank_in), (data_hbm, data_in), (select_hbm, select_ref), (shifts_hbm, shifts_ref)]
    loads = [pltpu.make_async_copy(src, dst, local_sems.at[i]) for i, (src, dst) in enumerate(inputs)]
    for load in loads:
        load.start()
    barrier = pltpu.get_barrier_semaphore()
    greeted = [in_depth(w) for w in along] + [in_group(q) for q in group]
    greeted += [{"tm": me, "sta": lax.rem(s + i, K)} for i in range(1, K)]
    for device in greeted:
        pl.semaphore_signal(barrier, inc=1, device_id=device, device_id_type=MESH)

    channels = data_in.shape[0]
    flip_at = lax.broadcasted_iota(jnp.int32, (B, B), 0) + lax.broadcasted_iota(jnp.int32, (B, B), 1)
    flip = jnp.where(flip_at == B - 1, 1.0, 0.0).astype(bf16)
    loads[0].wait()
    rows = bank_in[...].astype(f32)
    centred = rows - jnp.sum(rows, axis=1, keepdims=True) / TL
    power = jnp.sum(centred * centred, axis=1, keepdims=True)
    normed = (centred * lax.rsqrt(power + 1e-05)).astype(bf16)
    for b in range(TPL_ROWS):
        lay[pl.ds(b, channels, stride=TPL_ROWS), :] = dot(normed[:, b * B : (b + 1) * B], flip)
    bank_ref[...] = lay[: channels * TPL_ROWS].astype(bf16).reshape(bank_ref.shape)
    pl.semaphore_wait(barrier, len(greeted))

    for q in group:
        remote(bank_ref.at[pl.ds(q * per, per)], raw.at[p], bank_sems, in_group(q)).start()
    loads[1].wait()
    for a in range(PIECE):
        lay[pl.ds(a, channels, stride=PIECE), :] = data_in[:, a * B : (a + 1) * B].astype(f32)
    data_ref[...] = lay[...].astype(bf16).reshape(data_ref.shape)
    for q in group[::-1]:
        remote(data_ref.at[pl.ds(q * per, per)], rows_ref.at[p], data_sems, in_group(q)).start()
    raw[p] = bank_ref[pl.ds(p * per, per)]
    rows_ref[p] = data_ref[pl.ds(p * per, per)]

    loads[2].wait()
    loads[3].wait()
    bank_all = remote(raw.at[pl.ds(0, GROUP - 1)], raw.at[pl.ds(0, GROUP - 1)], bank_sems, self)
    bank_all.wait_recv()
    for k in range(K):
        offered = raw[lax.rem(select_ref[k], GROUP)]
        part[2 * k] = offered[:5]
        part[2 * k + 1] = offered[4:]
    for w in along:
        remote(part.at[w], got.at[z], part_sems, in_depth(w)).start()
    got[z] = part[z]

    data_all = remote(rows_ref.at[pl.ds(0, GROUP - 1)], rows_ref.at[pl.ds(0, GROUP - 1)], data_sems, self)
    data_all.wait_recv()
    halo = remote(rows_ref.at[0], rows_ref.at[GROUP], halo_sems, in_depth(lax.rem(z + depth - 1, depth)))
    halo.start()

    part_all = remote(got.at[pl.ds(0, depth - 1)], got.at[pl.ds(0, depth - 1)], part_sems, self)
    part_all.wait_recv()
    tpl_ref[z] = got[lax.div(select_ref[lax.div(z, 2)], GROUP)]
    for w in along:
        tpl_copy(z, in_depth(w)).start()

    part_row = lax.broadcasted_iota(jnp.int32, (16, B), 0)
    part_lane = lax.broadcasted_iota(jnp.int32, (16, B), 1)
    zero = jnp.zeros((16, B), f32)

    def spread_one(tpl, c, k):
        tpl = tpl.astype(f32)
        lines = [jnp.broadcast_to(tpl[m : m + 1], (16, B)) for m in range(TPL_ROWS)]
        for g in range(0, B, 16):
            wraps = part_lane - part_row < 1 + g
            turned = [pltpu.roll(line, 1 + g, axis=1, stride=1, stride_axis=0) for line in lines]
            turned = [zero] + turned + [zero]
            for b in range(LAGS):
                block = jnp.where(wraps, turned[b + 1], turned[b])
                toeplitz[c, k, b * B + g : b * B + g + 16] = block.astype(bf16)

    def spread(w):
        k = lax.div(w, 2)
        half = w - 2 * k
        for i in range(4):
            spread_one(tpl_ref[w, i + half], 5 * half + i, k)

        @pl.when(half == 0)
        def _():
            spread_one(tpl_ref[w, 4], 4, k)

    spread(z)

    halo.wait_recv()
    row = lax.broadcasted_iota(jnp.int32, (ALL_ROWS, B), 0)
    before = lax.broadcasted_iota(jnp.int32, (B, 2 * B), 0) < lax.broadcasted_iota(jnp.int32, (B, 2 * B), 1)
    sums = jnp.where(before, 1.0, 0.0).astype(bf16)
    valid = jnp.where(z == depth - 1, OUT_ROWS, ALL_ROWS)

    def prepare(c, carry):
        x = jnp.where(row < valid, rows_ref[:, c].astype(f32).reshape(ALL_ROWS, B), 0.0)
        x_ref[...] = x
        square = x * x
        high = square.astype(bf16)
        low = (square - high.astype(f32)).astype(bf16)
        window_sum = windows(dot(x.astype(bf16), sums))
        window_sq = windows(dot(high, sums) + dot(low, sums))
        scales[c] = lax.rsqrt(jnp.maximum(window_sq - window_sum * window_sum / TL, TL / 8.0))
        series[c] = jnp.concatenate([x_ref[b : b + ROWS] for b in range(LAGS)], axis=1).astype(bf16)
        return carry

    lax.fori_loop(0, per, prepare, 0)
    stack[...] = jnp.zeros_like(stack)

    lane = lax.broadcasted_iota(jnp.int32, (OUT_ROWS, B), 1)

    def arrive(i, carry):
        away = jnp.where(lax.rem(i, 2) == 1, lax.div(i + 1, 2), depth - lax.div(i, 2))
        w = lax.rem(z + away, depth)
        tpl_copy(w, self).wait_recv()
        spread(w)
        return carry

    lax.fori_loop(1, depth, arrive, 0)

    def correlate(c):
        return dot(series[c], jnp.concatenate([toeplitz[c, k] for k in range(K)], axis=1))

    def add(c, k, correl):
        shift = shifts_ref[k, p * per + c]
        far = shift >= B
        rest = jnp.where(far, shift - B, shift)
        turned = pltpu.roll(correl[:, k * B : (k + 1) * B] * scales[c], jnp.where(rest == 0, 0, B - rest), axis=1)
        first, second, third = turned[:OUT_ROWS], turned[1 : OUT_ROWS + 1], turned[2 : OUT_ROWS + 2]
        near_sum = jnp.where(lane < B - rest, first, second)
        far_sum = jnp.where(lane < B - rest, second, third)
        stack[k] += jnp.where(far, far_sum, near_sum).reshape(GROUP, PIECE, B)

    def channel(c, carry):
        correl = correlate(c)
        for k in range(K):
            add(c, k, correl)
        return carry

    lax.fori_loop(0, per - 1, channel, 0, unroll=True)

    correl = correlate(per - 1)
    for k in range(K):
        add(per - 1, k, correl)
        for dz, dy, dx in steps:
            if dz == 0:
                q = neighbour(dy, dx)
                remote(stack.at[k, q], from_all.at[p * K + s], stack_sems, {"tm": z * GROUP + q, "sta": k}).start()

        @pl.when(s != k)
        def _():
            remote(stack.at[k, p], from_all.at[p * K + s], stack_sems, {"tm": me, "sta": k}).start()

    from_all[p * K + s] = stack[s, p]
    senders = GROUP * K - 1
    stack_all = remote(from_all.at[pl.ds(0, senders)], from_all.at[pl.ds(0, senders)], stack_sems, self)
    stack_all.wait_recv()
    total = from_all[0]
    for j in range(1, GROUP * K):
        total += from_all[j]
    peaks[pl.ds(me, 1)] = jnp.max(jnp.abs(total), axis=0, keepdims=True)

    mine = peaks.at[pl.ds(me, 1)]
    for dz, dy, dx in steps:
        device = {"tm": lax.rem(z + dz, depth) * GROUP + neighbour(dy, dx), "sta": s}
        remote(mine, mine, peak_sems, device).start()
    peak_all = remote(peaks.at[pl.ds(0, count - 1)], peaks.at[pl.ds(0, count - 1)], peak_sems, self)
    peak_all.wait_recv()
    out_ref[...] = total / (jnp.max(peaks[...]) + 1e-06)
    tpl_all = pltpu.make_async_copy(tpl_ref.at[pl.ds(0, depth - 1)], tpl_ref.at[pl.ds(0, depth - 1)], tpl_sent)
    tpl_all.wait()
    for sent in (bank_all, data_all, part_all, halo, stack_all, peak_all):
        sent.wait_send()


def on_device(data, bank, select, shifts):
    channels = data.shape[0]
    per = channels // GROUP
    tpl_parts = (2 * K, 5, TPL_ROWS, B)
    hbm = pl.BlockSpec(memory_space=pltpu.HBM)
    out = pl.pallas_call(
        kernel,
        out_shape=jax.ShapeDtypeStruct((PIECE, B), f32),
        in_specs=[hbm] * 4,
        out_specs=pl.BlockSpec(memory_space=pltpu.VMEM),
        scratch_shapes=[
            pltpu.SMEM(select.shape, jnp.int32),
            pltpu.SMEM(shifts.shape, jnp.int32),
            pltpu.VMEM(data.shape, bf16),
            pltpu.VMEM(bank.shape[1:], bf16),
            pltpu.VMEM((channels * PIECE, B), f32),
            pltpu.VMEM((channels, PIECE, B), bf16),
            pltpu.VMEM((channels, TPL_ROWS, B), bf16),
            pltpu.VMEM((GROUP + 1, per, PIECE, B), bf16),
            pltpu.VMEM((GROUP, per, TPL_ROWS, B), bf16),
            pltpu.VMEM(tpl_parts, bf16),
            pltpu.VMEM(tpl_parts, bf16),
            pltpu.VMEM(tpl_parts, bf16),
            pltpu.VMEM((ALL_ROWS, B), f32),
            pltpu.VMEM((per, ROWS, B), f32),
            pltpu.VMEM((per, ROWS, LAGS * B), bf16),
            pltpu.VMEM((per, K, LAGS * B, B), bf16),
            pltpu.VMEM((K, GROUP, PIECE, B), f32),
            pltpu.VMEM((GROUP * K, PIECE, B), f32),
            pltpu.VMEM((lax.axis_size("tm"), B), f32),
            pltpu.SemaphoreType.DMA((4,)),
        ]
        + [pltpu.SemaphoreType.DMA((2,))] * 6
        + [pltpu.SemaphoreType.DMA, pltpu.SemaphoreType.DMA((2 * K,))],
        compiler_params=pltpu.CompilerParams(
            collective_id=0, has_side_effects=True, vmem_limit_bytes=int(53.8 * 2**20)
        ),
    )(select, data, bank, shifts)
    return out.reshape(1, PIECE * B)


def solution(mesh):
    in_specs = (P("sta", "tm"), P("tm", "sta", None), P(), P(None, "sta"))
    out_specs = P("sta", "tm")
    return jax.shard_map(on_device, mesh=mesh, in_specs=in_specs, out_specs=out_specs, check_vma=False)
```
